128 devices in a mesh: row: 8 (over x, core), col: 16 (over y, z).
Axes of the slice: x: 4, y: 4, z: 4, core: 2. Of those that a mesh axis runs over, the one named last changes fastest.
Arguments:
- momentum: float32 [8192, 28672], P('row', 'col'), may hold values from -200 to 200
- gradient: bfloat16 [8192, 28672], P('row', 'col'), may hold values from -6 to 6
- weight: bfloat16 [8192, 28672], P('row', 'col'), may hold values from -6 to 6
- basis_prev: float32 [8192, 512], P('row'), may hold values from -0.0625 to 0.0625
Outputs:
- new_momentum: float32 [8192, 28672], P('row', 'col')
- new_basis: float32 [8192, 512], P('row')
- new_weight: bfloat16 [8192, 28672], P('row', 'col')
The draws below stay inside these ranges and needn't reach their ends.
All inputs are finite; a program needn't handle non-finite values.
Results may differ from the reference program's by a relative error of at most 0.001.
Values sent between devices are 32-bit elements; how exact they have to be, the bound alone decides.
No kernel may reach another device: no remote copies, remote signals or barrier semaphores. Data moves between devices by JAX's collectives and lax.ppermute only.
A program may use at most 128 MiB of HBM per device.

```python
import math
import jax
import jax.numpy as jnp
from jax import lax

D = 8192
FF = 28672
RANK = 512


def draw_momentum(key, part):
    key = jax.random.fold_in(key, 11)
    key_base, key_rows, key_cols = jax.random.split(key, 3)
    row_pos = jnp.arange(D, dtype=jnp.float32)[:, None] / D
    col_pos = jnp.arange(FF, dtype=jnp.float32)[None, :] / FF
    col_scale = jnp.exp(jax.random.uniform(key_cols, (1, FF), jnp.float32, 0.0, math.log(10.0)) + math.log(3.0) * col_pos)
    base = jnp.clip(jax.random.normal(key_base, (D, FF), jnp.float32), -6.0, 6.0)
    row_scale = jnp.exp(jax.random.uniform(key_rows, (D, 1), jnp.float32, 0.0, math.log(10.0)) + math.log(3.0) * row_pos)
    return base * row_scale * col_scale / 30.0


def levels(rng, extent, cuts, smallest, largest):
    def one(dim, parts):
        draws = jax.random.uniform(jax.random.fold_in(jax.random.fold_in(rng, 6), dim), (parts,), jnp.float32, smallest / len(cuts), largest / len(cuts))
        return jnp.repeat(jnp.exp(draws), extent[dim] // parts).reshape((-1,) + (1,) * (len(extent) - dim - 1))

    gain = one(*cuts[0])
    for cut in cuts[1:]:
        gain = gain * one(*cut)
    return gain


def centred(rng, extent, scale, reach, shards=(), kind=jnp.bfloat16):
    result = jax.random.normal(rng, extent, jnp.float32) * scale
    if len(shards) > 0:
        result = levels(rng, extent, shards, -0.22, 0.18) * result
    return jnp.clip(result, min=-reach, max=reach).astype(kind)


def setup_inputs(seed: int = 0) -> dict:
    keys = jax.random.split(jax.random.key(seed), 5)
    momentum = draw_momentum(jax.random.fold_in(keys[4], 71), 0)
    gradient = centred(keys[1], (D, FF), 1.0, 6.0, ((0, 8), (1, 16)))
    weight = centred(keys[2], (D, FF), 1.0, 6.0, ((0, 8), (1, 16)))
    basis_prev = centred(keys[3], (D, RANK), D ** -0.5, 0.0625, ((0, 8),), jnp.float32)
    return dict(momentum=momentum, gradient=gradient, weight=weight, basis_prev=basis_prev)


decay_keep = 0.95
step_rms = 0.2
norm_eps = 1e-06
highest = lax.Precision.HIGHEST

def reference(momentum, gradient, weight, basis_prev):
    blended = momentum + gradient.astype(jnp.float32)
    left_full = lax.dot_general(blended.astype(jnp.float32), basis_prev.astype(jnp.float32), (((0,), (0,)), ((), ())), precision=highest, preferred_element_type=jnp.float32)
    gram_sum = lax.dot_general(left_full.astype(jnp.float32), left_full.astype(jnp.float32), (((0,), (0,)), ((), ())), precision=highest, preferred_element_type=jnp.float32)
    factor = jnp.linalg.cholesky(gram_sum)
    ortho_left = jax.scipy.linalg.solve_triangular(factor, left_full.T, lower=True).T
    right_full = jnp.dot(blended.astype(jnp.float32), ortho_left.astype(jnp.float32), precision=highest, preferred_element_type=jnp.float32)
    new_momentum = blended - (1.0 - decay_keep) * jnp.dot(right_full.astype(jnp.float32), ortho_left.T.astype(jnp.float32), precision=highest, preferred_element_type=jnp.float32)
    squares = lax.optimization_barrier(jnp.sum(right_full * right_full, axis=0))
    new_basis = right_full / jnp.sqrt(squares + norm_eps)
    scale_step = step_rms * math.sqrt(D * FF / RANK)
    update = jnp.dot(new_basis.astype(jnp.float32), ortho_left.T.astype(jnp.float32), precision=highest, preferred_element_type=jnp.float32)
    new_weight = (weight.astype(jnp.float32) - scale_step * update).astype(jnp.bfloat16)
    return (new_momentum, new_basis, new_weight)
```

```python
import math

import jax
import jax.numpy as jnp
from jax import lax
from jax.experimental import pallas as pl
from jax.experimental.pallas import tpu as pltpu
from jax.sharding import PartitionSpec as P

D = 8192
FF = 28672
RANK = 512

decay_keep = 0.95
step_rms = 0.2
norm_eps = 1e-06
highest = lax.Precision.HIGHEST
high = lax.Precision.HIGH
block = 128


def dot(first, second, dims, precision):
    return lax.dot_general(
        first, second, ((dims[:1], dims[1:]), ((), ())), precision=precision, preferred_element_type=jnp.float32
    )


other_core = [(i, i ^ 1) for i in range(8)]


def along_x(shift):
    return [(2 * x + core, 2 * ((x + shift) % 4) + core) for x in range(4) for core in range(2)]


def along_y(shift):
    return [(4 * y + z, 4 * ((y + shift) % 4) + z) for y in range(4) for z in range(4)]


def along_z(shift):
    return [(4 * y + z, 4 * y + (z + shift) % 4) for y in range(4) for z in range(4)]


def pick(array, index, size):
    return lax.dynamic_slice_in_dim(array, index * size, size, 0)


def total(own, got):
    return (own + got[1]) + (got[0] + got[2])


def ring_sum(array, axis, moves):
    return total(array, [lax.ppermute(array, axis, moves(s)) for s in (1, 2, 3)])


def ring_scatter(array, axis, place, moves):
    size = array.shape[0] // 4
    got = [lax.ppermute(pick(array, (place + s) % 4, size), axis, moves(s)) for s in (1, 2, 3)]
    return total(pick(array, place, size), got)


def ring_gather(array, axis, place, moves):
    size = array.shape[0]
    parts = [array] + [lax.ppermute(array, axis, moves(s)) for s in (1, 2, 3)]
    whole = jnp.zeros((4 * size,) + array.shape[1:], array.dtype)
    for s, part in enumerate(parts):
        whole = lax.dynamic_update_slice_in_dim(whole, part, (place - s) % 4 * size, 0)
    return whole


def core_scatter(array, core):
    half = array.shape[0] // 2
    return pick(array, core, half) + lax.ppermute(pick(array, 1 - core, half), "row", other_core)


def core_gather(array, core):
    half = array.shape[0]
    whole = jnp.zeros((2 * half,) + array.shape[1:], array.dtype)
    whole = lax.dynamic_update_slice_in_dim(whole, array, core * half, 0)
    return lax.dynamic_update_slice_in_dim(whole, lax.ppermute(array, "row", other_core), (1 - core) * half, 0)


def invert_factor(square):
    size = square.shape[0]
    rows = lax.broadcasted_iota(jnp.int32, (8, size), 0)
    down = lax.broadcasted_iota(jnp.int32, (size, size), 0)
    across = lax.broadcasted_iota(jnp.int32, (size, size), 1)
    rest, image, done = square, jnp.where(down == across, 1.0, 0.0).astype(jnp.float32), []
    for first in range(0, size, 8):
        count = size - first
        cols = [jnp.broadcast_to(rest[:, first + j : first + j + 1], (count, size)) for j in range(8)]
        top, top_image = rest[:8], image[:8]
        rest, image = rest[8:], image[8:]
        for k in range(8):
            scale = lax.rsqrt(cols[k][k : k + 1, :])
            col = cols[k] * scale
            row, row_image = top[k : k + 1, :] * scale, top_image[k : k + 1, :] * scale
            top_image = jnp.where(rows == k, row_image, top_image)
            below = jnp.where(rows > k, col[:8], 0.0)
            top = top - below * row
            top_image = top_image - below * row_image
            if count > 8:
                rest = rest - col[8:] * row
                image = image - col[8:] * row_image
            for j in range(k + 1, 8):
                cols[j] = cols[j] - col * col[j : j + 1, :]
        done.append(top_image)
    return jnp.concatenate(done, axis=0)


def inverse_kernel(gram_ref, out_ref, left_ref, image_ref):
    left_ref[...] = gram_ref[...]
    image_ref[...] = jnp.zeros_like(image_ref)
    out_ref[...] = jnp.zeros_like(out_ref)
    for low in range(0, RANK, block):
        top = low + block
        corner = invert_factor(left_ref[low:top, low:top])
        out_ref[low:top, low:top] = corner
        if low:
            out_ref[low:top, :low] = dot(corner, image_ref[low:top, :low], (1, 0), highest)
        if top < RANK:
            panel = dot(left_ref[top:, low:top], corner, (1, 1), highest)
            for at in range(top, RANK, block):
                part = panel[at - top :]
                left_ref[at:, at : at + block] -= dot(part, part[:block], (1, 1), highest)
            image_ref[top:, :top] -= dot(panel, out_ref[low:top, :top], (1, 0), highest)


def inverse_of_factor(gram_sum):
    square = jax.ShapeDtypeStruct((RANK, RANK), jnp.float32)
    return pl.pallas_call(
        inverse_kernel,
        out_shape=square,
        scratch_shapes=[pltpu.VMEM((RANK, RANK), jnp.float32)] * 2,
        compiler_params=pltpu.CompilerParams(vmem_limit_bytes=32 * 2**20),
        cost_estimate=pl.CostEstimate(flops=2 * RANK**3, bytes_accessed=8 * RANK**2, transcendentals=RANK),
        name="inverse_of_factor",
    )(gram_sum)


def on_device(momentum, gradient, weight, basis_prev):
    row, col = lax.axis_index("row"), lax.axis_index("col")
    x, core, y, z = row // 2, row % 2, col // 4, col % 4
    blended = momentum + gradient.astype(jnp.float32)
    left_part = dot(blended, basis_prev, (0, 0), high)
    left_rows = ring_scatter(core_scatter(left_part, core), "row", x, along_x)
    left_full = core_gather(ring_gather(left_rows, "row", x, along_x), core)
    own = pick(dot(lax.dynamic_slice_in_dim(left_full, x * block, block, 1), left_full, (0, 0), highest), core, 64)
    gram_rows = ring_sum(ring_sum(own, "col", along_z), "col", along_y)
    gram_sum = ring_gather(core_gather(gram_rows, core), "row", x, along_x)
    product = dot(blended, left_full, (1, 0), high)
    first = ring_scatter(ring_scatter(product[:512], "col", z, along_z), "col", y, along_y)
    second = ring_scatter(ring_scatter(product[512:], "col", y, along_y), "col", z, along_z)
    first = ring_gather(ring_gather(first, "col", y, along_y), "col", z, along_z)
    second = ring_gather(ring_gather(second, "col", z, along_z), "col", y, along_y)
    inverse = inverse_of_factor(gram_sum)
    ortho_left = dot(left_full, inverse, (1, 1), high)
    right_full = dot(jnp.concatenate([first, second], 0), inverse, (1, 1), high)
    squares = jnp.sum(right_full * right_full, axis=0, keepdims=True)
    squares = squares + lax.ppermute(squares, "row", other_core)
    squares = ring_sum(squares, "row", along_x)
    new_momentum = blended - (1.0 - decay_keep) * dot(right_full, ortho_left, (1, 1), high)
    new_basis = right_full / jnp.sqrt(squares + norm_eps)
    scale_step = step_rms * math.sqrt(D * FF / RANK)
    update = dot(new_basis, ortho_left, (1, 1), high)
    new_weight = (weight.astype(jnp.float32) - scale_step * update).astype(jnp.bfloat16)
    return (new_momentum, new_basis, new_weight)


def solution(mesh):
    return jax.shard_map(
        on_device,
        mesh=mesh,
        in_specs=(P("row", "col"), P("row", "col"), P("row", "col"), P("row", None)),
        out_specs=(P("row", "col"), P("row", None), P("row", "col")),
        check_vma=False,
    )
```

```python
import math

import jax
import jax.numpy as jnp
from jax import lax
from jax.experimental import pallas as pl
from jax.experimental.pallas import tpu as pltpu
from jax.sharding import PartitionSpec as P

D = 8192
FF = 28672
RANK = 512

decay_keep = 0.95
step_rms = 0.2
norm_eps = 1e-06
highest = lax.Precision.HIGHEST
high = lax.Precision.HIGH
block = 128


def dot(first, second, dims, precision):
    return lax.dot_general(
        first, second, ((dims[:1], dims[1:]), ((), ())), precision=precision, preferred_element_type=jnp.float32
    )


other_core = [(i, i ^ 1) for i in range(8)]


def along_x(shift):
    return [(2 * x + core, 2 * ((x + shift) % 4) + core) for x in range(4) for core in range(2)]


def along_y(shift):
    return [(4 * y + z, 4 * ((y + shift) % 4) + z) for y in range(4) for z in range(4)]


def along_z(shift):
    return [(4 * y + z, 4 * y + (z + shift) % 4) for y in range(4) for z in range(4)]


def pick(array, index, size):
    return lax.dynamic_slice_in_dim(array, index * size, size, 0)


def total(own, got):
    return (own + got[1]) + (got[0] + got[2])


def ring_sum(array, axis, moves):
    return total(array, [lax.ppermute(array, axis, moves(s)) for s in (1, 2, 3)])


def ring_scatter(array, axis, place, moves):
    size = array.shape[0] // 4
    got = [lax.ppermute(pick(array, (place + s) % 4, size), axis, moves(s)) for s in (1, 2, 3)]
    return total(pick(array, place, size), got)


def ring_gather(array, axis, place, moves):
    size = array.shape[0]
    parts = [array] + [lax.ppermute(array, axis, moves(s)) for s in (1, 2, 3)]
    whole = jnp.zeros((4 * size,) + array.shape[1:], array.dtype)
    for s, part in enumerate(parts):
        whole = lax.dynamic_update_slice_in_dim(whole, part, (place - s) % 4 * size, 0)
    return whole


def core_scatter(array, core):
    half = array.shape[0] // 2
    return pick(array, core, half) + lax.ppermute(pick(array, 1 - core, half), "row", other_core)


def core_gather(array, core):
    half = array.shape[0]
    whole = jnp.zeros((2 * half,) + array.shape[1:], array.dtype)
    whole = lax.dynamic_update_slice_in_dim(whole, array, core * half, 0)
    return lax.dynamic_update_slice_in_dim(whole, lax.ppermute(array, "row", other_core), (1 - core) * half, 0)


def ring_parts(array, moves):
    return [array] + [lax.ppermute(array, "row", moves(s)) for s in (1, 2, 3)]


def invert_factor(square):
    size = square.shape[0]
    rows = lax.broadcasted_iota(jnp.int32, (8, size), 0)
    down = lax.broadcasted_iota(jnp.int32, (size, size), 0)
    across = lax.broadcasted_iota(jnp.int32, (size, size), 1)
    rest, image, done = square, jnp.where(down == across, 1.0, 0.0).astype(jnp.float32), []
    for first in range(0, size, 8):
        count = size - first
        cols = [jnp.broadcast_to(rest[:, first + j : first + j + 1], (count, size)) for j in range(8)]
        top, top_image = rest[:8], image[:8]
        rest, image = rest[8:], image[8:]
        for k in range(8):
            scale = lax.rsqrt(cols[k][k : k + 1, :])
            col = cols[k] * scale
            row, row_image = top[k : k + 1, :] * scale, top_image[k : k + 1, :] * scale
            top_image = jnp.where(rows == k, row_image, top_image)
            below = jnp.where(rows > k, col[:8], 0.0)
            top = top - below * row
            top_image = top_image - below * row_image
            if count > 8:
                rest = rest - col[8:] * row
                image = image - col[8:] * row_image
            for j in range(k + 1, 8):
                cols[j] = cols[j] - col * col[j : j + 1, :]
        done.append(top_image)
    return jnp.concatenate(done, axis=0)


def inverse_kernel(gram_ref, out_ref, left_ref, image_ref):
    left_ref[...] = gram_ref[...]
    image_ref[...] = jnp.zeros_like(image_ref)
    out_ref[...] = jnp.zeros_like(out_ref)
    for low in range(0, RANK, block):
        top = low + block
        corner = invert_factor(left_ref[low:top, low:top])
        out_ref[low:top, low:top] = corner
        if low:
            out_ref[low:top, :low] = dot(corner, image_ref[low:top, :low], (1, 0), highest)
        if top < RANK:
            panel = dot(left_ref[top:, low:top], corner, (1, 1), highest)
            for at in range(top, RANK, block):
                part = panel[at - top :]
                left_ref[at:, at : at + block] -= dot(part, part[:block], (1, 1), highest)
            image_ref[top:, :top] -= dot(panel, out_ref[low:top, :top], (1, 0), highest)


def inverse_of_factor(gram_sum):
    square = jax.ShapeDtypeStruct((RANK, RANK), jnp.float32)
    return pl.pallas_call(
        inverse_kernel,
        out_shape=square,
        scratch_shapes=[pltpu.VMEM((RANK, RANK), jnp.float32)] * 2,
        compiler_params=pltpu.CompilerParams(vmem_limit_bytes=32 * 2**20),
        cost_estimate=pl.CostEstimate(flops=2 * RANK**3, bytes_accessed=8 * RANK**2, transcendentals=RANK),
        name="inverse_of_factor",
    )(gram_sum)


def exchange(array):
    return lax.all_to_all(array, "col", 0, 0)


def col_scatter(array):
    return jnp.sum(exchange(array.reshape((16, array.shape[0] // 16) + array.shape[1:])), axis=0)


def col_gather(array):
    return exchange(jnp.broadcast_to(array[None], (16,) + array.shape)).reshape((16 * array.shape[0],) + array.shape[1:])


def split(array):
    high_part = array.astype(jnp.bfloat16)
    return high_part, (array - high_part.astype(jnp.float32)).astype(jnp.bfloat16)


def dot16(first, second, dims):
    return lax.dot_general(first, second, ((dims[:1], dims[1:]), ((), ())), preferred_element_type=jnp.float32)


def dot_split(first, second, dims):
    return dot16(first[0], second[0], dims) + (dot16(first[0], second[1], dims) + dot16(first[1], second[0], dims))


def call(kernel, grid, in_specs, out_specs, out_shape, scratch, flops, moved, name):
    return pl.pallas_call(
        kernel,
        grid=grid,
        in_specs=in_specs,
        out_specs=out_specs,
        out_shape=out_shape,
        scratch_shapes=scratch,
        compiler_params=pltpu.CompilerParams(vmem_limit_bytes=48 * 2**20),
        cost_estimate=pl.CostEstimate(flops=flops, bytes_accessed=moved, transcendentals=0),
        name=name,
    )


def tall(rows, columns):
    return pl.BlockSpec((rows, columns), lambda i: (i, 0))


def whole(*shape):
    return pl.BlockSpec(shape, lambda i: (0,) * len(shape), pipeline_mode=pl.Buffered(1))


def left_kernel(half_ref, momentum_ref, gradient_ref, basis_ref, out_ref, total_ref):
    step = pl.program_id(0)

    @pl.when(step == 0)
    def _():
        total_ref[...] = jnp.zeros_like(total_ref)

    blended = split(momentum_ref[...] + gradient_ref[...].astype(jnp.float32))
    total_ref[...] += dot_split(split(basis_ref[...]), blended, (0, 0))

    @pl.when(step == pl.num_programs(0) - 1)
    def _():
        out_ref[...] = total_ref[...].T


def left_half(half, momentum, gradient, basis_prev):
    rows, columns = momentum.shape
    tile, width = 256, columns // 2
    piece = pl.BlockSpec((tile, width), lambda i, half: (i, half[0]))
    return pl.pallas_call(
        left_kernel,
        grid_spec=pltpu.PrefetchScalarGridSpec(
            num_scalar_prefetch=1,
            grid=(rows // tile,),
            in_specs=[piece, piece, pl.BlockSpec((tile, RANK), lambda i, half: (i, 0))],
            out_specs=pl.BlockSpec((width, RANK), lambda i, half: (0, 0)),
            scratch_shapes=[pltpu.VMEM((RANK, width), jnp.float32)],
        ),
        out_shape=jax.ShapeDtypeStruct((width, RANK), jnp.float32),
        compiler_params=pltpu.CompilerParams(vmem_limit_bytes=48 * 2**20),
        cost_estimate=pl.CostEstimate(
            flops=6 * rows * width * RANK, bytes_accessed=6 * rows * width + 8 * width * RANK, transcendentals=0
        ),
        name="left_half",
    )(half, momentum, gradient, basis_prev)


def product_kernel(place_ref, momentum_ref, gradient_ref, *refs):
    parts, (product_ref, left_ref, high_ref, low_ref) = refs[:8], refs[8:]

    @pl.when(pl.program_id(0) == 0)
    def _():
        x, core = place_ref[0], place_ref[1]
        for i, part in enumerate(parts):
            at = 4 * (core if i < 4 else 1 - core) + (x + 4 - i % 4) % 4
            value = part[...]
            left_ref[at] = value
            high_ref[at], low_ref[at] = split(value)

    count = left_ref.shape[0] * left_ref.shape[1]
    left = [ref[...].reshape(count, RANK) for ref in (high_ref, low_ref)]
    blended = split(momentum_ref[...] + gradient_ref[...].astype(jnp.float32))
    product_ref[...] = dot_split(blended, left, (1, 0))


def blended_times_left(place, momentum, gradient, parts):
    rows, columns = momentum.shape
    tile, size = 256, parts[0].shape[0]
    shape = (8, size, RANK)
    return call(
        product_kernel,
        (rows // tile,),
        [pl.BlockSpec(memory_space=pltpu.SMEM), tall(tile, columns), tall(tile, columns)] + [whole(size, RANK)] * 8,
        [tall(tile, RANK), whole(*shape)],
        [jax.ShapeDtypeStruct((rows, RANK), jnp.float32), jax.ShapeDtypeStruct(shape, jnp.float32)],
        [pltpu.VMEM(shape, jnp.bfloat16)] * 2,
        6 * rows * columns * RANK,
        6 * rows * columns + 8 * columns * RANK,
        "blended_times_left",
    )(place, momentum, gradient, *parts)


def ortho_kernel(left_ref, inverse_ref, high_ref, low_ref, inverse_high_ref, inverse_low_ref):
    @pl.when(pl.program_id(0) == 0)
    def _():
        inverse_high_ref[...], inverse_low_ref[...] = split(inverse_ref[...])

    inverse = inverse_high_ref[...], inverse_low_ref[...]
    high_ref[...], low_ref[...] = split(dot_split(inverse, split(left_ref[...]), (1, 1)))


def ortho_halves(left_full, inverse):
    columns, tile = left_full.shape[0], 256
    return call(
        ortho_kernel,
        (columns // tile,),
        [tall(tile, RANK), whole(RANK, RANK)],
        [pl.BlockSpec((RANK, tile), lambda i: (0, i))] * 2,
        [jax.ShapeDtypeStruct((RANK, columns), jnp.bfloat16)] * 2,
        [pltpu.VMEM((RANK, RANK), jnp.bfloat16)] * 2,
        6 * columns * RANK**2,
        8 * columns * RANK,
        "ortho_halves",
    )(left_full, inverse)


def right_kernel(product_ref, inverse_ref, right_ref, squares_ref, inverse_high_ref, inverse_low_ref):
    @pl.when(pl.program_id(0) == 0)
    def _():
        inverse_high_ref[...], inverse_low_ref[...] = split(inverse_ref[...])
        squares_ref[...] = jnp.zeros_like(squares_ref)

    right = dot_split(split(product_ref[...]), (inverse_high_ref[...], inverse_low_ref[...]), (1, 1))
    right_ref[...] = right
    squares_ref[...] += jnp.sum(right * right, axis=0, keepdims=True)


def right_and_squares(product_full, inverse):
    rows, tile = product_full.shape[0], 256
    return call(
        right_kernel,
        (rows // tile,),
        [tall(tile, RANK), whole(RANK, RANK)],
        [tall(tile, RANK), whole(1, RANK)],
        [jax.ShapeDtypeStruct((rows, RANK), jnp.float32), jax.ShapeDtypeStruct((1, RANK), jnp.float32)],
        [pltpu.VMEM((RANK, RANK), jnp.bfloat16)] * 2,
        6 * rows * RANK**2,
        8 * rows * RANK,
        "right_and_squares",
    )(product_full, inverse)


def momentum_kernel(right_ref, ortho_ref, momentum_ref, gradient_ref, out_ref):
    projection = dot16(right_ref[...].astype(jnp.bfloat16), ortho_ref[...], (1, 0))
    out_ref[...] = momentum_ref[...] + gradient_ref[...].astype(jnp.float32) - (1.0 - decay_keep) * projection


def next_momentum(right_full, ortho_high, momentum, gradient):
    rows, columns = momentum.shape
    tile = 256
    return call(
        momentum_kernel,
        (rows // tile,),
        [tall(tile, RANK), whole(RANK, columns), tall(tile, columns), tall(tile, columns)],
        tall(tile, columns),
        jax.ShapeDtypeStruct((rows, columns), jnp.float32),
        [],
        2 * rows * columns * RANK,
        10 * rows * columns,
        "next_momentum",
    )(right_full, ortho_high, momentum, gradient)


def weight_kernel(right_ref, squares_ref, high_ref, low_ref, weight_ref, basis_ref, out_ref):
    basis = right_ref[...] / jnp.sqrt(squares_ref[...] + norm_eps)
    basis_ref[...] = basis
    update = dot_split(split(basis), (high_ref[...], low_ref[...]), (1, 0))
    scale_step = step_rms * math.sqrt(D * FF / RANK)
    out_ref[...] = (weight_ref[...].astype(jnp.float32) - scale_step * update).astype(jnp.bfloat16)


def next_weight(right_full, squares, ortho, weight):
    rows, columns = weight.shape
    tile = 512
    return call(
        weight_kernel,
        (rows // tile,),
        [tall(tile, RANK), whole(1, RANK), whole(RANK, columns), whole(RANK, columns), tall(tile, columns)],
        [tall(tile, RANK), tall(tile, columns)],
        [jax.ShapeDtypeStruct((rows, RANK), jnp.float32), jax.ShapeDtypeStruct((rows, columns), jnp.bfloat16)],
        [],
        6 * rows * columns * RANK,
        4 * rows * columns + 8 * rows * RANK,
        "next_weight",
    )(right_full, squares, *ortho, weight)


def exchange(array):
    return lax.all_to_all(array, "col", 0, 0)


def col_scatter(array):
    return jnp.sum(exchange(array.reshape((16, array.shape[0] // 16) + array.shape[1:])), axis=0)


def col_gather(array):
    return exchange(jnp.broadcast_to(array[None], (16,) + array.shape)).reshape((16 * array.shape[0],) + array.shape[1:])


def on_device(momentum, gradient, weight, basis_prev):
    row, col = lax.axis_index("row"), lax.axis_index("col")
    x, core, y, z = row // 2, row % 2, col // 4, col % 4
    given = left_half(jnp.reshape(1 - core, (1,)).astype(jnp.int32), momentum, gradient, basis_prev)
    taken = lax.ppermute(given, "row", other_core)
    kept = left_half(jnp.reshape(core, (1,)).astype(jnp.int32), momentum, gradient, basis_prev)
    left_rows = ring_scatter(kept + taken, "row", x, along_x)

    parts = ring_parts(left_rows, along_x)
    gram_rows = core_scatter(dot(left_rows, left_rows, (0, 0), highest), core)
    gram_rows = ring_scatter(ring_scatter(gram_rows, "col", y, along_y), "col", z, along_z)
    parts, gram_rows = lax.optimization_barrier((parts, gram_rows))
    parts = parts + [lax.ppermute(part, "row", other_core) for part in parts]
    place = jnp.stack([x, core]).astype(jnp.int32)
    product, left_full = blended_times_left(place, momentum, gradient, parts)
    left_full = left_full.reshape(-1, RANK)
    got = ring_parts(gram_rows, along_x)
    product, got = lax.optimization_barrier((product, got))
    gram_rows = total(got[0], got[1:])

    count = gram_rows.shape[0]
    gram_copies = jnp.broadcast_to(gram_rows[None], (16,) + gram_rows.shape)
    mixed = exchange(jnp.concatenate([gram_copies, product.reshape(16, -1, RANK)], 1))
    product_full = col_gather(jnp.sum(mixed[:, count:], axis=0))
    inverse = inverse_of_factor(core_gather(mixed[:, :count].reshape(-1, RANK), core))
    ortho = ortho_halves(left_full, inverse)
    ortho, product_full = lax.optimization_barrier((ortho, product_full))

    right_full, squares = right_and_squares(product_full, inverse)
    squares = squares + lax.ppermute(squares, "row", other_core)
    squares = ring_sum(squares, "row", along_x)
    new_momentum = next_momentum(right_full, ortho[0], momentum, gradient)
    new_basis, new_weight = next_weight(right_full, squares, ortho, weight)
    return (new_momentum, new_basis, new_weight)


def solution(mesh):
    return jax.shard_map(
        on_device,
        mesh=mesh,
        in_specs=(P("row", "col"), P("row", "col"), P("row", "col"), P("row", None)),
        out_specs=(P("row", "col"), P("row", None), P("row", "col")),
        check_vma=False,
    )
```

```python
import math

import jax
import jax.numpy as jnp
from jax import lax
from jax.experimental import pallas as pl
from jax.experimental.pallas import tpu as pltpu
from jax.sharding import PartitionSpec as P

D = 8192
FF = 28672
RANK = 512

decay_keep = 0.95
step_rms = 0.2
norm_eps = 1e-06
highest = lax.Precision.HIGHEST
high = lax.Precision.HIGH
block = 128


def dot(first, second, dims, precision):
    return lax.dot_general(
        first, second, ((dims[:1], dims[1:]), ((), ())), precision=precision, preferred_element_type=jnp.float32
    )


other_core = [(i, i ^ 1) for i in range(8)]


def along_x(shift):
    return [(2 * x + core, 2 * ((x + shift) % 4) + core) for x in range(4) for core in range(2)]


def along_y(shift):
    return [(4 * y + z, 4 * ((y + shift) % 4) + z) for y in range(4) for z in range(4)]


def along_z(shift):
    return [(4 * y + z, 4 * y + (z + shift) % 4) for y in range(4) for z in range(4)]


def pick(array, index, size):
    return lax.dynamic_slice_in_dim(array, index * size, size, 0)


def total(own, got):
    return (own + got[1]) + (got[0] + got[2])


def ring_sum(array, axis, moves):
    return total(array, [lax.ppermute(array, axis, moves(s)) for s in (1, 2, 3)])


def ring_scatter(array, axis, place, moves):
    size = array.shape[0] // 4
    got = [lax.ppermute(pick(array, (place + s) % 4, size), axis, moves(s)) for s in (1, 2, 3)]
    return total(pick(array, place, size), got)


def ring_gather(array, axis, place, moves):
    size = array.shape[0]
    parts = [array] + [lax.ppermute(array, axis, moves(s)) for s in (1, 2, 3)]
    whole = jnp.zeros((4 * size,) + array.shape[1:], array.dtype)
    for s, part in enumerate(parts):
        whole = lax.dynamic_update_slice_in_dim(whole, part, (place - s) % 4 * size, 0)
    return whole


def core_scatter(array, core):
    half = array.shape[0] // 2
    return pick(array, core, half) + lax.ppermute(pick(array, 1 - core, half), "row", other_core)


def core_gather(array, core):
    half = array.shape[0]
    whole = jnp.zeros((2 * half,) + array.shape[1:], array.dtype)
    whole = lax.dynamic_update_slice_in_dim(whole, array, core * half, 0)
    return lax.dynamic_update_slice_in_dim(whole, lax.ppermute(array, "row", other_core), (1 - core) * half, 0)


def ring_parts(array, moves):
    return [array] + [lax.ppermute(array, "row", moves(s)) for s in (1, 2, 3)]


def invert_factor(square):
    size = square.shape[0]
    rows = lax.broadcasted_iota(jnp.int32, (8, size), 0)
    down = lax.broadcasted_iota(jnp.int32, (size, size), 0)
    across = lax.broadcasted_iota(jnp.int32, (size, size), 1)
    rest, image, done = square, jnp.where(down == across, 1.0, 0.0).astype(jnp.float32), []
    for first in range(0, size, 8):
        count = size - first
        cols = [jnp.broadcast_to(rest[:, first + j : first + j + 1], (count, size)) for j in range(8)]
        top, top_image = rest[:8], image[:8]
        rest, image = rest[8:], image[8:]
        for k in range(8):
            scale = lax.rsqrt(cols[k][k : k + 1, :])
            col = cols[k] * scale
            row, row_image = top[k : k + 1, :] * scale, top_image[k : k + 1, :] * scale
            top_image = jnp.where(rows == k, row_image, top_image)
            below = jnp.where(rows > k, col[:8], 0.0)
            top = top - below * row
            top_image = top_image - below * row_image
            if count > 8:
                rest = rest - col[8:] * row
                image = image - col[8:] * row_image
            for j in range(k + 1, 8):
                cols[j] = cols[j] - col * col[j : j + 1, :]
        done.append(top_image)
    return jnp.concatenate(done, axis=0)


def inverse_kernel(gram_ref, out_ref, left_ref, image_ref):
    left_ref[...] = gram_ref[...]
    image_ref[...] = jnp.zeros_like(image_ref)
    out_ref[...] = jnp.zeros_like(out_ref)
    for low in range(0, RANK, block):
        top = low + block
        corner = invert_factor(left_ref[low:top, low:top])
        out_ref[low:top, low:top] = corner
        if low:
            out_ref[low:top, :low] = dot(corner, image_ref[low:top, :low], (1, 0), highest)
        if top < RANK:
            panel = dot(left_ref[top:, low:top], corner, (1, 1), highest)
            for at in range(top, RANK, block):
                part = panel[at - top :]
                left_ref[at:, at : at + block] -= dot(part, part[:block], (1, 1), highest)
            image_ref[top:, :top] -= dot(panel, out_ref[low:top, :top], (1, 0), highest)


def inverse_of_factor(gram_sum):
    square = jax.ShapeDtypeStruct((RANK, RANK), jnp.float32)
    return pl.pallas_call(
        inverse_kernel,
        out_shape=square,
        scratch_shapes=[pltpu.VMEM((RANK, RANK), jnp.float32)] * 2,
        compiler_params=pltpu.CompilerParams(vmem_limit_bytes=32 * 2**20),
        cost_estimate=pl.CostEstimate(flops=2 * RANK**3, bytes_accessed=8 * RANK**2, transcendentals=RANK),
        name="inverse_of_factor",
    )(gram_sum)


def exchange(array):
    return lax.all_to_all(array, "col", 0, 0)


def col_scatter(array):
    return jnp.sum(exchange(array.reshape((16, array.shape[0] // 16) + array.shape[1:])), axis=0)


def col_gather(array):
    return exchange(jnp.broadcast_to(array[None], (16,) + array.shape)).reshape((16 * array.shape[0],) + array.shape[1:])


def split(array):
    high_part = array.astype(jnp.bfloat16)
    return high_part, (array - high_part.astype(jnp.float32)).astype(jnp.bfloat16)


def dot16(first, second, dims):
    return lax.dot_general(first, second, ((dims[:1], dims[1:]), ((), ())), preferred_element_type=jnp.float32)


def dot_split(first, second, dims):
    return dot16(first[0], second[0], dims) + (dot16(first[0], second[1], dims) + dot16(first[1], second[0], dims))


def call(kernel, grid, in_specs, out_specs, out_shape, scratch, flops, moved, name, room):
    return pl.pallas_call(
        kernel,
        grid=grid,
        in_specs=in_specs,
        out_specs=out_specs,
        out_shape=out_shape,
        scratch_shapes=scratch,
        compiler_params=pltpu.CompilerParams(vmem_limit_bytes=room * 2**20),
        cost_estimate=pl.CostEstimate(flops=flops, bytes_accessed=moved, transcendentals=0),
        name=name,
    )


def tall(rows, columns):
    return pl.BlockSpec((rows, columns), lambda i: (i, 0))


def whole(*shape):
    return pl.BlockSpec(shape, lambda i: (0,) * len(shape), pipeline_mode=pl.Buffered(1))


def left_kernel(half_ref, momentum_ref, gradient_ref, basis_ref, left_ref):
    blended = split(momentum_ref[...] + gradient_ref[...].astype(jnp.float32))
    part = dot_split(blended, split(basis_ref[...]), (0, 0))

    @pl.when(pl.program_id(0) == 0)
    def _():
        left_ref[...] = part

    @pl.when(pl.program_id(0) > 0)
    def _():
        left_ref[...] += part


def left_half(half, momentum, gradient, basis_prev):
    rows, columns = momentum.shape
    tile, width = 512, columns // 2
    piece = pl.BlockSpec((tile, width), lambda i, half: (i, half[0]))
    return pl.pallas_call(
        left_kernel,
        grid_spec=pltpu.PrefetchScalarGridSpec(
            num_scalar_prefetch=1,
            grid=(rows // tile,),
            in_specs=[piece, piece, pl.BlockSpec((tile, RANK), lambda i, half: (i, 0))],
            out_specs=pl.BlockSpec((width, RANK), lambda i, half: (0, 0)),
        ),
        out_shape=jax.ShapeDtypeStruct((width, RANK), jnp.float32),
        compiler_params=pltpu.CompilerParams(vmem_limit_bytes=54 * 2**20),
        cost_estimate=pl.CostEstimate(
            flops=6 * rows * width * RANK, bytes_accessed=6 * rows * width + 8 * width * RANK, transcendentals=0
        ),
        name="left_half",
    )(half, momentum, gradient, basis_prev)


def product_kernel(place_ref, momentum_ref, gradient_ref, *refs):
    parts, (product_ref, left_ref, high_ref, low_ref) = refs[:8], refs[8:]

    @pl.when(pl.program_id(0) == 0)
    def _():
        x, core = place_ref[0], place_ref[1]
        for i, part in enumerate(parts):
            at = 4 * (core if i < 4 else 1 - core) + (x + 4 - i % 4) % 4
            value = part[...]
            left_ref[at] = value
            high_ref[at], low_ref[at] = split(value)

    count = left_ref.shape[0] * left_ref.shape[1]
    left = [ref[...].reshape(count, RANK) for ref in (high_ref, low_ref)]
    blended = split(momentum_ref[...] + gradient_ref[...].astype(jnp.float32))
    product_ref[...] = dot_split(blended, left, (1, 0))


def blended_times_left(place, momentum, gradient, parts):
    rows, columns = momentum.shape
    tile, size = 256, parts[0].shape[0]
    shape = (8, size, RANK)
    return call(
        product_kernel,
        (rows // tile,),
        [pl.BlockSpec(memory_space=pltpu.SMEM), tall(tile, columns), tall(tile, columns)] + [whole(size, RANK)] * 8,
        [tall(tile, RANK), whole(*shape)],
        [jax.ShapeDtypeStruct((rows, RANK), jnp.float32), jax.ShapeDtypeStruct(shape, jnp.float32)],
        [pltpu.VMEM(shape, jnp.bfloat16)] * 2,
        6 * rows * columns * RANK,
        6 * rows * columns + 8 * columns * RANK,
        "blended_times_left",
        48,
    )(place, momentum, gradient, *parts)


def ortho_kernel(left_ref, inverse_ref, high_ref, low_ref, inverse_high_ref, inverse_low_ref):
    @pl.when(pl.program_id(0) == 0)
    def _():
        inverse_high_ref[...], inverse_low_ref[...] = split(inverse_ref[...])

    inverse = inverse_high_ref[...], inverse_low_ref[...]
    high_ref[...], low_ref[...] = split(dot_split(inverse, split(left_ref[...]), (1, 1)))


def ortho_halves(left_full, inverse):
    columns, tile = left_full.shape[0], 256
    return call(
        ortho_kernel,
        (columns // tile,),
        [tall(tile, RANK), whole(RANK, RANK)],
        [pl.BlockSpec((RANK, tile), lambda i: (0, i))] * 2,
        [jax.ShapeDtypeStruct((RANK, columns), jnp.bfloat16)] * 2,
        [pltpu.VMEM((RANK, RANK), jnp.bfloat16)] * 2,
        6 * columns * RANK**2,
        8 * columns * RANK,
        "ortho_halves",
        12,
    )(left_full, inverse)


def right_kernel(product_ref, inverse_ref, right_ref, squares_ref, inverse_high_ref, inverse_low_ref):
    @pl.when(pl.program_id(0) == 0)
    def _():
        inverse_high_ref[...], inverse_low_ref[...] = split(inverse_ref[...])
        squares_ref[...] = jnp.zeros_like(squares_ref)

    right = dot_split(split(product_ref[...]), (inverse_high_ref[...], inverse_low_ref[...]), (1, 1))
    right_ref[...] = right
    squares_ref[...] += jnp.sum(right * right, axis=0, keepdims=True)


def right_and_squares(product_full, inverse):
    rows, tile = product_full.shape[0], 256
    return call(
        right_kernel,
        (rows // tile,),
        [tall(tile, RANK), whole(RANK, RANK)],
        [tall(tile, RANK), whole(1, RANK)],
        [jax.ShapeDtypeStruct((rows, RANK), jnp.float32), jax.ShapeDtypeStruct((1, RANK), jnp.float32)],
        [pltpu.VMEM((RANK, RANK), jnp.bfloat16)] * 2,
        6 * rows * RANK**2,
        8 * rows * RANK,
        "right_and_squares",
        12,
    )(product_full, inverse)


def momentum_kernel(right_ref, ortho_ref, momentum_ref, gradient_ref, out_ref):
    projection = dot16(right_ref[...].astype(jnp.bfloat16), ortho_ref[...], (1, 0))
    out_ref[...] = momentum_ref[...] + gradient_ref[...].astype(jnp.float32) - (1.0 - decay_keep) * projection


def next_momentum(right_full, ortho_high, momentum, gradient):
    rows, columns = momentum.shape
    tile = 256
    return call(
        momentum_kernel,
        (rows // tile,),
        [tall(tile, RANK), whole(RANK, columns), tall(tile, columns), tall(tile, columns)],
        tall(tile, columns),
        jax.ShapeDtypeStruct((rows, columns), jnp.float32),
        [],
        2 * rows * columns * RANK,
        10 * rows * columns,
        "next_momentum",
        20,
    )(right_full, ortho_high, momentum, gradient)


def weight_kernel(right_ref, squares_ref, high_ref, low_ref, weight_ref, basis_ref, out_ref):
    basis = right_ref[...] / jnp.sqrt(squares_ref[...] + norm_eps)
    basis_ref[...] = basis
    update = dot_split(split(basis), (high_ref[...], low_ref[...]), (1, 0))
    scale_step = step_rms * math.sqrt(D * FF / RANK)
    out_ref[...] = (weight_ref[...].astype(jnp.float32) - scale_step * update).astype(jnp.bfloat16)


def next_weight(right_full, squares, ortho, weight):
    rows, columns = weight.shape
    tile = 256
    return call(
        weight_kernel,
        (rows // tile,),
        [tall(tile, RANK), whole(1, RANK), whole(RANK, columns), whole(RANK, columns), tall(tile, columns)],
        [tall(tile, RANK), tall(tile, columns)],
        [jax.ShapeDtypeStruct((rows, RANK), jnp.float32), jax.ShapeDtypeStruct((rows, columns), jnp.bfloat16)],
        [],
        6 * rows * columns * RANK,
        4 * rows * columns + 8 * rows * RANK,
        "next_weight",
        24,
    )(right_full, squares, *ortho, weight)


def exchange(array):
    return lax.all_to_all(array, "col", 0, 0)


def col_scatter(array):
    return jnp.sum(exchange(array.reshape((16, array.shape[0] // 16) + array.shape[1:])), axis=0)


def col_gather(array):
    return exchange(jnp.broadcast_to(array[None], (16,) + array.shape)).reshape((16 * array.shape[0],) + array.shape[1:])


def on_device(momentum, gradient, weight, basis_prev):
    row, col = lax.axis_index("row"), lax.axis_index("col")
    x, core, y, z = row // 2, row % 2, col // 4, col % 4
    given = left_half(jnp.reshape(1 - core, (1,)).astype(jnp.int32), momentum, gradient, basis_prev)
    taken = lax.ppermute(given, "row", other_core)
    kept = left_half(jnp.reshape(core, (1,)).astype(jnp.int32), momentum, gradient, basis_prev)
    left_rows = ring_scatter(kept + taken, "row", x, along_x)

    parts = ring_parts(left_rows, along_x)
    gram_rows = core_scatter(dot(left_rows, left_rows, (0, 0), highest), core)
    gram_rows = ring_scatter(ring_scatter(gram_rows, "col", y, along_y), "col", z, along_z)
    parts, gram_rows = lax.optimization_barrier((parts, gram_rows))
    parts = parts + [lax.ppermute(part, "row", other_core) for part in parts]
    place = jnp.stack([x, core]).astype(jnp.int32)
    product, left_full = blended_times_left(place, momentum, gradient, parts)
    left_full = left_full.reshape(-1, RANK)
    got = ring_parts(gram_rows, along_x)
    product, got = lax.optimization_barrier((product, got))
    gram_rows = total(got[0], got[1:])

    count = gram_rows.shape[0]
    gram_copies = jnp.broadcast_to(gram_rows[None], (16,) + gram_rows.shape)
    mixed = exchange(jnp.concatenate([gram_copies, product.reshape(16, -1, RANK)], 1))
    product_full = col_gather(jnp.sum(mixed[:, count:], axis=0))
    inverse = inverse_of_factor(core_gather(mixed[:, :count].reshape(-1, RANK), core))
    ortho = ortho_halves(left_full, inverse)
    ortho, product_full = lax.optimization_barrier((ortho, product_full))

    right_full, squares = right_and_squares(product_full, inverse)
    squares = squares + lax.ppermute(squares, "row", other_core)
    squares = ring_sum(squares, "row", along_x)
    new_momentum = next_momentum(right_full, ortho[0], momentum, gradient)
    new_basis, new_weight = next_weight(right_full, squares, ortho, weight)
    return (new_momentum, new_basis, new_weight)


def solution(mesh):
    return jax.shard_map(
        on_device,
        mesh=mesh,
        in_specs=(P("row", "col"), P("row", "col"), P("row", "col"), P("row", None)),
        out_specs=(P("row", "col"), P("row", None), P("row", "col")),
        check_vma=False,
    )
```

```python
import math

import jax
import jax.numpy as jnp
from jax import lax
from jax.experimental import pallas as pl
from jax.experimental.pallas import tpu as pltpu
from jax.sharding import PartitionSpec as P

D = 8192
FF = 28672
RANK = 512

decay_keep = 0.95
step_rms = 0.2
norm_eps = 1e-06
highest = lax.Precision.HIGHEST
high = lax.Precision.HIGH
block = 128


def dot(first, second, dims, precision):
    return lax.dot_general(
        first, second, ((dims[:1], dims[1:]), ((), ())), precision=precision, preferred_element_type=jnp.float32
    )


other_core = [(i, i ^ 1) for i in range(8)]


def along_x(shift):
    return [(2 * x + core, 2 * ((x + shift) % 4) + core) for x in range(4) for core in range(2)]


def along_y(shift):
    return [(4 * y + z, 4 * ((y + shift) % 4) + z) for y in range(4) for z in range(4)]


def along_z(shift):
    return [(4 * y + z, 4 * y + (z + shift) % 4) for y in range(4) for z in range(4)]


def pick(array, index, size):
    return lax.dynamic_slice_in_dim(array, index * size, size, 0)


def total(own, got):
    return (own + got[1]) + (got[0] + got[2])


def ring_sum(array, axis, moves):
    return total(array, [lax.ppermute(array, axis, moves(s)) for s in (1, 2, 3)])


def ring_scatter(array, axis, place, moves):
    size = array.shape[0] // 4
    got = [lax.ppermute(pick(array, (place + s) % 4, size), axis, moves(s)) for s in (1, 2, 3)]
    return total(pick(array, place, size), got)


def ring_gather(array, axis, place, moves):
    size = array.shape[0]
    parts = [array] + [lax.ppermute(array, axis, moves(s)) for s in (1, 2, 3)]
    whole = jnp.zeros((4 * size,) + array.shape[1:], array.dtype)
    for s, part in enumerate(parts):
        whole = lax.dynamic_update_slice_in_dim(whole, part, (place - s) % 4 * size, 0)
    return whole


def core_scatter(array, core):
    half = array.shape[0] // 2
    return pick(array, core, half) + lax.ppermute(pick(array, 1 - core, half), "row", other_core)


def core_gather(array, core):
    half = array.shape[0]
    whole = jnp.zeros((2 * half,) + array.shape[1:], array.dtype)
    whole = lax.dynamic_update_slice_in_dim(whole, array, core * half, 0)
    return lax.dynamic_update_slice_in_dim(whole, lax.ppermute(array, "row", other_core), (1 - core) * half, 0)


def ring_parts(array, moves):
    return [array] + [lax.ppermute(array, "row", moves(s)) for s in (1, 2, 3)]


def invert_factor(square):
    size = square.shape[0]
    rows = lax.broadcasted_iota(jnp.int32, (8, size), 0)
    down = lax.broadcasted_iota(jnp.int32, (size, size), 0)
    across = lax.broadcasted_iota(jnp.int32, (size, size), 1)
    rest, image, done = square, jnp.where(down == across, 1.0, 0.0).astype(jnp.float32), []
    for first in range(0, size, 8):
        count = size - first
        cols = [jnp.broadcast_to(rest[:, first + j : first + j + 1], (count, size)) for j in range(8)]
        top, top_image = rest[:8], image[:8]
        rest, image = rest[8:], image[8:]
        for k in range(8):
            scale = lax.rsqrt(cols[k][k : k + 1, :])
            col = cols[k] * scale
            row, row_image = top[k : k + 1, :] * scale, top_image[k : k + 1, :] * scale
            top_image = jnp.where(rows == k, row_image, top_image)
            below = jnp.where(rows > k, col[:8], 0.0)
            top = top - below * row
            top_image = top_image - below * row_image
            if count > 8:
                rest = rest - col[8:] * row
                image = image - col[8:] * row_image
            for j in range(k + 1, 8):
                cols[j] = cols[j] - col * col[j : j + 1, :]
        done.append(top_image)
    return jnp.concatenate(done, axis=0)


def inverse_kernel(gram_ref, out_ref, left_ref, image_ref):
    left_ref[...] = gram_ref[...]
    image_ref[...] = jnp.zeros_like(image_ref)
    out_ref[...] = jnp.zeros_like(out_ref)
    for low in range(0, RANK, block):
        top = low + block
        corner = invert_factor(left_ref[low:top, low:top])
        out_ref[low:top, low:top] = corner
        if low:
            out_ref[low:top, :low] = dot(corner, image_ref[low:top, :low], (1, 0), highest)
        if top < RANK:
            panel = dot(left_ref[top:, low:top], corner, (1, 1), highest)
            for at in range(top, RANK, block):
                part = panel[at - top :]
                left_ref[at:, at : at + block] -= dot(part, part[:block], (1, 1), highest)
            image_ref[top:, :top] -= dot(panel, out_ref[low:top, :top], (1, 0), highest)


def inverse_of_factor(gram_sum):
    square = jax.ShapeDtypeStruct((RANK, RANK), jnp.float32)
    return pl.pallas_call(
        inverse_kernel,
        out_shape=square,
        scratch_shapes=[pltpu.VMEM((RANK, RANK), jnp.float32)] * 2,
        compiler_params=pltpu.CompilerParams(vmem_limit_bytes=32 * 2**20),
        cost_estimate=pl.CostEstimate(flops=2 * RANK**3, bytes_accessed=8 * RANK**2, transcendentals=RANK),
        name="inverse_of_factor",
    )(gram_sum)


def exchange(array):
    return lax.all_to_all(array, "col", 0, 0)


def col_scatter(array):
    return jnp.sum(exchange(array.reshape((16, array.shape[0] // 16) + array.shape[1:])), axis=0)


def col_gather(array):
    return exchange(jnp.broadcast_to(array[None], (16,) + array.shape)).reshape((16 * array.shape[0],) + array.shape[1:])


def split(array):
    high_part = array.astype(jnp.bfloat16)
    return high_part, (array - high_part.astype(jnp.float32)).astype(jnp.bfloat16)


def dot16(first, second, dims):
    return lax.dot_general(first, second, ((dims[:1], dims[1:]), ((), ())), preferred_element_type=jnp.float32)


def dot_split(first, second, dims):
    return dot16(first[0], second[0], dims) + (dot16(first[0], second[1], dims) + dot16(first[1], second[0], dims))


def call(kernel, grid, in_specs, out_specs, out_shape, scratch, flops, moved, name, room):
    return pl.pallas_call(
        kernel,
        grid=grid,
        in_specs=in_specs,
        out_specs=out_specs,
        out_shape=out_shape,
        scratch_shapes=scratch,
        compiler_params=pltpu.CompilerParams(vmem_limit_bytes=room * 2**20),
        cost_estimate=pl.CostEstimate(flops=flops, bytes_accessed=moved, transcendentals=0),
        name=name,
    )


def tall(rows, columns):
    return pl.BlockSpec((rows, columns), lambda i: (i, 0))


def whole(*shape):
    return pl.BlockSpec(shape, lambda i: (0,) * len(shape), pipeline_mode=pl.Buffered(1))


def left_kernel(half_ref, momentum_ref, gradient_ref, basis_ref, left_ref):
    blended = split(momentum_ref[...] + gradient_ref[...].astype(jnp.float32))
    part = dot_split(blended, split(basis_ref[...]), (0, 0))

    @pl.when(pl.program_id(0) == 0)
    def _():
        left_ref[...] = part

    @pl.when(pl.program_id(0) > 0)
    def _():
        left_ref[...] += part


def left_half(half, momentum, gradient, basis_prev):
    rows, columns = momentum.shape
    tile, width = 512, columns // 2
    piece = pl.BlockSpec((tile, width), lambda i, half: (i, half[0]))
    return pl.pallas_call(
        left_kernel,
        grid_spec=pltpu.PrefetchScalarGridSpec(
            num_scalar_prefetch=1,
            grid=(rows // tile,),
            in_specs=[piece, piece, pl.BlockSpec((tile, RANK), lambda i, half: (i, 0))],
            out_specs=pl.BlockSpec((width, RANK), lambda i, half: (0, 0)),
        ),
        out_shape=jax.ShapeDtypeStruct((width, RANK), jnp.float32),
        compiler_params=pltpu.CompilerParams(vmem_limit_bytes=54 * 2**20),
        cost_estimate=pl.CostEstimate(
            flops=6 * rows * width * RANK, bytes_accessed=6 * rows * width + 8 * width * RANK, transcendentals=0
        ),
        name="left_half",
    )(half, momentum, gradient, basis_prev)


def product_kernel(place_ref, momentum_ref, gradient_ref, *refs):
    parts, (product_ref, left_ref, whole_ref, high_ref, low_ref) = refs[:8], refs[8:]

    @pl.when(pl.program_id(0) == 0)
    def _():
        x, core = place_ref[0], place_ref[1]
        for i, part in enumerate(parts):
            at = 4 * (core if i < 4 else 1 - core) + (x + 4 - i % 4) % 4
            value = part[...]
            whole_ref[at] = value
            high_ref[at], low_ref[at] = split(value)

    step, chunks = pl.program_id(0), left_ref.shape[0]
    left_ref[...] = whole_ref[pl.ds(step * chunks, chunks)]
    count = whole_ref.shape[0] * whole_ref.shape[1]
    left = [ref[...].reshape(count, RANK) for ref in (high_ref, low_ref)]
    blended = split(momentum_ref[...] + gradient_ref[...].astype(jnp.float32))
    product_ref[...] = dot_split(blended, left, (1, 0))


def blended_times_left(place, momentum, gradient, parts):
    rows, columns = momentum.shape
    tile, size = 256, parts[0].shape[0]
    shape = (8, size, RANK)
    return call(
        product_kernel,
        (rows // tile,),
        [pl.BlockSpec(memory_space=pltpu.SMEM), tall(tile, columns), tall(tile, columns)] + [whole(size, RANK)] * 8,
        [tall(tile, RANK), pl.BlockSpec((8 * tile // rows, size, RANK), lambda i: (i, 0, 0))],
        [jax.ShapeDtypeStruct((rows, RANK), jnp.float32), jax.ShapeDtypeStruct(shape, jnp.float32)],
        [pltpu.VMEM(shape, jnp.float32)] + [pltpu.VMEM(shape, jnp.bfloat16)] * 2,
        6 * rows * columns * RANK,
        6 * rows * columns + 8 * columns * RANK,
        "blended_times_left",
        48,
    )(place, momentum, gradient, *parts)


def ortho_kernel(left_ref, inverse_ref, high_ref, low_ref, inverse_high_ref, inverse_low_ref):
    @pl.when(pl.program_id(0) == 0)
    def _():
        inverse_high_ref[...], inverse_low_ref[...] = split(inverse_ref[...])

    inverse = inverse_high_ref[...], inverse_low_ref[...]
    high_ref[...], low_ref[...] = split(dot_split(inverse, split(left_ref[...]), (1, 1)))


def ortho_halves(left_full, inverse):
    columns, tile = left_full.shape[0], 256
    return call(
        ortho_kernel,
        (columns // tile,),
        [tall(tile, RANK), whole(RANK, RANK)],
        [pl.BlockSpec((RANK, tile), lambda i: (0, i))] * 2,
        [jax.ShapeDtypeStruct((RANK, columns), jnp.bfloat16)] * 2,
        [pltpu.VMEM((RANK, RANK), jnp.bfloat16)] * 2,
        6 * columns * RANK**2,
        8 * columns * RANK,
        "ortho_halves",
        12,
    )(left_full, inverse)


def right_kernel(product_ref, inverse_ref, right_ref, squares_ref, inverse_high_ref, inverse_low_ref):
    @pl.when(pl.program_id(0) == 0)
    def _():
        inverse_high_ref[...], inverse_low_ref[...] = split(inverse_ref[...])
        squares_ref[...] = jnp.zeros_like(squares_ref)

    right = dot_split(split(product_ref[...]), (inverse_high_ref[...], inverse_low_ref[...]), (1, 1))
    right_ref[...] = right
    squares_ref[...] += jnp.sum(right * right, axis=0, keepdims=True)


def right_and_squares(product_full, inverse):
    rows, tile = product_full.shape[0], 256
    return call(
        right_kernel,
        (rows // tile,),
        [tall(tile, RANK), whole(RANK, RANK)],
        [tall(tile, RANK), whole(1, RANK)],
        [jax.ShapeDtypeStruct((rows, RANK), jnp.float32), jax.ShapeDtypeStruct((1, RANK), jnp.float32)],
        [pltpu.VMEM((RANK, RANK), jnp.bfloat16)] * 2,
        6 * rows * RANK**2,
        8 * rows * RANK,
        "right_and_squares",
        12,
    )(product_full, inverse)


def momentum_kernel(right_ref, ortho_ref, momentum_ref, gradient_ref, out_ref):
    projection = dot16(right_ref[...].astype(jnp.bfloat16), ortho_ref[...], (1, 0))
    out_ref[...] = momentum_ref[...] + gradient_ref[...].astype(jnp.float32) - (1.0 - decay_keep) * projection


def next_momentum(right_full, ortho_high, momentum, gradient):
    rows, columns = momentum.shape
    tile = 256
    return call(
        momentum_kernel,
        (rows // tile,),
        [tall(tile, RANK), whole(RANK, columns), tall(tile, columns), tall(tile, columns)],
        tall(tile, columns),
        jax.ShapeDtypeStruct((rows, columns), jnp.float32),
        [],
        2 * rows * columns * RANK,
        10 * rows * columns,
        "next_momentum",
        20,
    )(right_full, ortho_high, momentum, gradient)


def weight_kernel(right_ref, squares_ref, high_ref, low_ref, weight_ref, basis_ref, out_ref):
    basis = right_ref[...] / jnp.sqrt(squares_ref[...] + norm_eps)
    basis_ref[...] = basis
    update = dot_split(split(basis), (high_ref[...], low_ref[...]), (1, 0))
    scale_step = step_rms * math.sqrt(D * FF / RANK)
    out_ref[...] = (weight_ref[...].astype(jnp.float32) - scale_step * update).astype(jnp.bfloat16)


def next_weight(right_full, squares, ortho, weight):
    rows, columns = weight.shape
    tile = 256
    return call(
        weight_kernel,
        (rows // tile,),
        [tall(tile, RANK), whole(1, RANK), whole(RANK, columns), whole(RANK, columns), tall(tile, columns)],
        [tall(tile, RANK), tall(tile, columns)],
        [jax.ShapeDtypeStruct((rows, RANK), jnp.float32), jax.ShapeDtypeStruct((rows, columns), jnp.bfloat16)],
        [],
        6 * rows * columns * RANK,
        4 * rows * columns + 8 * rows * RANK,
        "next_weight",
        24,
    )(right_full, squares, *ortho, weight)


def exchange(array):
    return lax.all_to_all(array, "col", 0, 0)


def col_scatter(array):
    return jnp.sum(exchange(array.reshape((16, array.shape[0] // 16) + array.shape[1:])), axis=0)


def col_gather(array):
    return exchange(jnp.broadcast_to(array[None], (16,) + array.shape)).reshape((16 * array.shape[0],) + array.shape[1:])


def on_device(momentum, gradient, weight, basis_prev):
    row, col = lax.axis_index("row"), lax.axis_index("col")
    x, core, y, z = row // 2, row % 2, col // 4, col % 4
    given = left_half(jnp.reshape(1 - core, (1,)).astype(jnp.int32), momentum, gradient, basis_prev)
    taken = lax.ppermute(given, "row", other_core)
    kept = left_half(jnp.reshape(core, (1,)).astype(jnp.int32), momentum, gradient, basis_prev)
    size = kept.shape[0] // 4
    sums = [pick(kept, (x + s) % 4, size) + pick(taken, (x + s) % 4, size) for s in range(4)]
    left_rows = total(sums[0], [lax.ppermute(sums[s], "row", along_x(s)) for s in (1, 2, 3)])

    parts = ring_parts(left_rows, along_x)
    gram_rows = core_scatter(dot(left_rows, left_rows, (0, 0), highest), core)
    gram_rows = ring_scatter(ring_scatter(gram_rows, "col", y, along_y), "col", z, along_z)
    parts, gram_rows = lax.optimization_barrier((parts, gram_rows))
    parts = parts + [lax.ppermute(part, "row", other_core) for part in parts]
    place = jnp.stack([x, core]).astype(jnp.int32)
    product, left_full = blended_times_left(place, momentum, gradient, parts)
    left_full = left_full.reshape(-1, RANK)
    got = ring_parts(gram_rows, along_x)
    product, got = lax.optimization_barrier((product, got))
    gram_rows = total(got[0], got[1:])

    count = gram_rows.shape[0]
    gram_copies = jnp.broadcast_to(gram_rows[None], (16,) + gram_rows.shape)
    mixed = exchange(jnp.concatenate([gram_copies, product.reshape(16, -1, RANK)], 1))
    product_full = col_gather(jnp.sum(mixed[:, count:], axis=0))
    inverse = inverse_of_factor(core_gather(mixed[:, :count].reshape(-1, RANK), core))
    ortho = ortho_halves(left_full, inverse)
    ortho, product_full = lax.optimization_barrier((ortho, product_full))

    right_full, squares = right_and_squares(product_full, inverse)
    squares = squares + lax.ppermute(squares, "row", other_core)
    squares = ring_sum(squares, "row", along_x)
    new_momentum = next_momentum(right_full, ortho[0], momentum, gradient)
    new_basis, new_weight = next_weight(right_full, squares, ortho, weight)
    return (new_momentum, new_basis, new_weight)


def solution(mesh):
    return jax.shard_map(
        on_device,
        mesh=mesh,
        in_specs=(P("row", "col"), P("row", "col"), P("row", "col"), P("row", None)),
        out_specs=(P("row", "col"), P("row", None), P("row", "col")),
        check_vma=False,
    )
```

```python
import math

import jax
import jax.numpy as jnp
from jax import lax
from jax.experimental import pallas as pl
from jax.experimental.pallas import tpu as pltpu
from jax.sharding import PartitionSpec as P

D = 8192
FF = 28672
RANK = 512

decay_keep = 0.95
step_rms = 0.2
norm_eps = 1e-06
highest = lax.Precision.HIGHEST
high = lax.Precision.HIGH
block = 128


def dot(first, second, dims, precision):
    return lax.dot_general(
        first, second, ((dims[:1], dims[1:]), ((), ())), precision=precision, preferred_element_type=jnp.float32
    )


other_core = [(i, i ^ 1) for i in range(8)]


def along_x(shift):
    return [(2 * x + core, 2 * ((x + shift) % 4) + core) for x in range(4) for core in range(2)]


def along_y(shift):
    return [(4 * y + z, 4 * ((y + shift) % 4) + z) for y in range(4) for z in range(4)]


def along_z(shift):
    return [(4 * y + z, 4 * y + (z + shift) % 4) for y in range(4) for z in range(4)]


def pick(array, index, size):
    return lax.dynamic_slice_in_dim(array, index * size, size, 0)


def total(own, got):
    return (own + got[1]) + (got[0] + got[2])


def ring_sum(array, axis, moves):
    return total(array, [lax.ppermute(array, axis, moves(s)) for s in (1, 2, 3)])


def ring_scatter(array, axis, place, moves):
    size = array.shape[0] // 4
    got = [lax.ppermute(pick(array, (place + s) % 4, size), axis, moves(s)) for s in (1, 2, 3)]
    return total(pick(array, place, size), got)


def ring_gather(array, axis, place, moves):
    size = array.shape[0]
    parts = [array] + [lax.ppermute(array, axis, moves(s)) for s in (1, 2, 3)]
    whole = jnp.zeros((4 * size,) + array.shape[1:], array.dtype)
    for s, part in enumerate(parts):
        whole = lax.dynamic_update_slice_in_dim(whole, part, (place - s) % 4 * size, 0)
    return whole


def core_scatter(array, core):
    half = array.shape[0] // 2
    return pick(array, core, half) + lax.ppermute(pick(array, 1 - core, half), "row", other_core)


def core_gather(array, core):
    half = array.shape[0]
    whole = jnp.zeros((2 * half,) + array.shape[1:], array.dtype)
    whole = lax.dynamic_update_slice_in_dim(whole, array, core * half, 0)
    return lax.dynamic_update_slice_in_dim(whole, lax.ppermute(array, "row", other_core), (1 - core) * half, 0)


def ring_parts(array, moves):
    return [array] + [lax.ppermute(array, "row", moves(s)) for s in (1, 2, 3)]


def invert_factor(square):
    size = square.shape[0]
    rows = lax.broadcasted_iota(jnp.int32, (8, size), 0)
    down = lax.broadcasted_iota(jnp.int32, (size, size), 0)
    across = lax.broadcasted_iota(jnp.int32, (size, size), 1)
    rest, image, done = square, jnp.where(down == across, 1.0, 0.0).astype(jnp.float32), []
    for first in range(0, size, 8):
        count = size - first
        cols = [jnp.broadcast_to(rest[:, first + j : first + j + 1], (count, size)) for j in range(8)]
        top, top_image = rest[:8], image[:8]
        rest, image = rest[8:], image[8:]
        for k in range(8):
            scale = lax.rsqrt(cols[k][k : k + 1, :])
            col = cols[k] * scale
            row, row_image = top[k : k + 1, :] * scale, top_image[k : k + 1, :] * scale
            top_image = jnp.where(rows == k, row_image, top_image)
            below = jnp.where(rows > k, col[:8], 0.0)
            top = top - below * row
            top_image = top_image - below * row_image
            if count > 8:
                rest = rest - col[8:] * row
                image = image - col[8:] * row_image
            for j in range(k + 1, 8):
                cols[j] = cols[j] - col * col[j : j + 1, :]
        done.append(top_image)
    return jnp.concatenate(done, axis=0)


def inverse_kernel(gram_ref, out_ref, left_ref, image_ref):
    left_ref[...] = gram_ref[...]
    image_ref[...] = jnp.zeros_like(image_ref)
    out_ref[...] = jnp.zeros_like(out_ref)
    for low in range(0, RANK, block):
        top = low + block
        corner = invert_factor(left_ref[low:top, low:top])
        out_ref[low:top, low:top] = corner
        if low:
            out_ref[low:top, :low] = dot(corner, image_ref[low:top, :low], (1, 0), highest)
        if top < RANK:
            panel = dot(left_ref[top:, low:top], corner, (1, 1), highest)
            for at in range(top, RANK, block):
                part = panel[at - top :]
                left_ref[at:, at : at + block] -= dot(part, part[:block], (1, 1), highest)
            image_ref[top:, :top] -= dot(panel, out_ref[low:top, :top], (1, 0), highest)


def inverse_of_factor(gram_sum):
    square = jax.ShapeDtypeStruct((RANK, RANK), jnp.float32)
    return pl.pallas_call(
        inverse_kernel,
        out_shape=square,
        scratch_shapes=[pltpu.VMEM((RANK, RANK), jnp.float32)] * 2,
        compiler_params=pltpu.CompilerParams(vmem_limit_bytes=12 * 2**20),
        cost_estimate=pl.CostEstimate(flops=24 * RANK**3, bytes_accessed=8 * RANK**2, transcendentals=RANK),
        name="inverse_of_factor",
    )(gram_sum)


def exchange(array):
    return lax.all_to_all(array, "col", 0, 0)


def col_scatter(array):
    return jnp.sum(exchange(array.reshape((16, array.shape[0] // 16) + array.shape[1:])), axis=0)


def col_gather(array):
    return exchange(jnp.broadcast_to(array[None], (16,) + array.shape)).reshape((16 * array.shape[0],) + array.shape[1:])


def split(array):
    high_part = array.astype(jnp.bfloat16)
    return high_part, (array - high_part.astype(jnp.float32)).astype(jnp.bfloat16)


def dot16(first, second, dims):
    return lax.dot_general(first, second, ((dims[:1], dims[1:]), ((), ())), preferred_element_type=jnp.float32)


def dot_split(first, second, dims):
    return dot16(first[0], second[0], dims) + (dot16(first[0], second[1], dims) + dot16(first[1], second[0], dims))


def call(kernel, grid, in_specs, out_specs, out_shape, scratch, flops, moved, name, room):
    return pl.pallas_call(
        kernel,
        grid=grid,
        in_specs=in_specs,
        out_specs=out_specs,
        out_shape=out_shape,
        scratch_shapes=scratch,
        compiler_params=pltpu.CompilerParams(vmem_limit_bytes=room * 2**20),
        cost_estimate=pl.CostEstimate(flops=flops, bytes_accessed=moved, transcendentals=0),
        name=name,
    )


def tall(rows, columns):
    return pl.BlockSpec((rows, columns), lambda i: (i, 0))


def whole(*shape):
    return pl.BlockSpec(shape, lambda i: (0,) * len(shape), pipeline_mode=pl.Buffered(1))


def left_kernel(half_ref, momentum_ref, gradient_ref, basis_ref, left_ref):
    blended = split(momentum_ref[...] + gradient_ref[...].astype(jnp.float32))
    part = dot_split(blended, split(basis_ref[...]), (0, 0))

    @pl.when(pl.program_id(0) == 0)
    def _():
        left_ref[...] = part

    @pl.when(pl.program_id(0) > 0)
    def _():
        left_ref[...] += part


def left_half(half, momentum, gradient, basis_prev):
    rows, columns = momentum.shape
    tile, width = 512, columns // 2
    piece = pl.BlockSpec((tile, width), lambda i, half: (i, half[0]))
    return pl.pallas_call(
        left_kernel,
        grid_spec=pltpu.PrefetchScalarGridSpec(
            num_scalar_prefetch=1,
            grid=(rows // tile,),
            in_specs=[piece, piece, pl.BlockSpec((tile, RANK), lambda i, half: (i, 0))],
            out_specs=pl.BlockSpec((width, RANK), lambda i, half: (0, 0)),
        ),
        out_shape=jax.ShapeDtypeStruct((width, RANK), jnp.float32),
        compiler_params=pltpu.CompilerParams(vmem_limit_bytes=54 * 2**20),
        cost_estimate=pl.CostEstimate(
            flops=6 * rows * width * RANK, bytes_accessed=6 * rows * width + 8 * width * RANK, transcendentals=0
        ),
        name="left_half",
    )(half, momentum, gradient, basis_prev)


def product_kernel(place_ref, momentum_ref, gradient_ref, *refs):
    parts, (product_ref, left_ref, whole_ref, high_ref, low_ref) = refs[:8], refs[8:]

    @pl.when(pl.program_id(0) == 0)
    def _():
        x, core = place_ref[0], place_ref[1]
        for i, part in enumerate(parts):
            at = 4 * (core if i < 4 else 1 - core) + (x + 4 - i % 4) % 4
            value = part[...]
            whole_ref[at] = value
            high_ref[at], low_ref[at] = split(value)

    step, chunks = pl.program_id(0), left_ref.shape[0]
    left_ref[...] = whole_ref[pl.ds(step * chunks, chunks)]
    count = whole_ref.shape[0] * whole_ref.shape[1]
    left = [ref[...].reshape(count, RANK) for ref in (high_ref, low_ref)]
    blended = split(momentum_ref[...] + gradient_ref[...].astype(jnp.float32))
    product_ref[...] = dot_split(blended, left, (1, 0))


def blended_times_left(place, momentum, gradient, parts):
    rows, columns = momentum.shape
    tile, size = 256, parts[0].shape[0]
    shape = (8, size, RANK)
    return call(
        product_kernel,
        (rows // tile,),
        [pl.BlockSpec(memory_space=pltpu.SMEM), tall(tile, columns), tall(tile, columns)] + [whole(size, RANK)] * 8,
        [tall(tile, RANK), pl.BlockSpec((8 * tile // rows, size, RANK), lambda i: (i, 0, 0))],
        [jax.ShapeDtypeStruct((rows, RANK), jnp.float32), jax.ShapeDtypeStruct(shape, jnp.float32)],
        [pltpu.VMEM(shape, jnp.float32)] + [pltpu.VMEM(shape, jnp.bfloat16)] * 2,
        6 * rows * columns * RANK,
        6 * rows * columns + 8 * columns * RANK,
        "blended_times_left",
        48,
    )(place, momentum, gradient, *parts)


def ortho_kernel(left_ref, inverse_ref, high_ref, low_ref, inverse_high_ref, inverse_low_ref):
    @pl.when(pl.program_id(0) == 0)
    def _():
        inverse_high_ref[...], inverse_low_ref[...] = split(inverse_ref[...])

    inverse = inverse_high_ref[...], inverse_low_ref[...]
    high_ref[...], low_ref[...] = split(dot_split(inverse, split(left_ref[...]), (1, 1)))


def ortho_halves(left_full, inverse):
    columns, tile = left_full.shape[0], 256
    return call(
        ortho_kernel,
        (columns // tile,),
        [tall(tile, RANK), whole(RANK, RANK)],
        [pl.BlockSpec((RANK, tile), lambda i: (0, i))] * 2,
        [jax.ShapeDtypeStruct((RANK, columns), jnp.bfloat16)] * 2,
        [pltpu.VMEM((RANK, RANK), jnp.bfloat16)] * 2,
        6 * columns * RANK**2,
        8 * columns * RANK,
        "ortho_halves",
        12,
    )(left_full, inverse)


def right_kernel(product_ref, inverse_ref, right_ref, squares_ref, inverse_high_ref, inverse_low_ref):
    @pl.when(pl.program_id(0) == 0)
    def _():
        inverse_high_ref[...], inverse_low_ref[...] = split(inverse_ref[...])
        squares_ref[...] = jnp.zeros_like(squares_ref)

    right = dot_split(split(product_ref[...]), (inverse_high_ref[...], inverse_low_ref[...]), (1, 1))
    right_ref[...] = right
    squares_ref[...] += jnp.sum(right * right, axis=0, keepdims=True)


def right_and_squares(product_full, inverse):
    rows, tile = product_full.shape[0], 256
    return call(
        right_kernel,
        (rows // tile,),
        [tall(tile, RANK), whole(RANK, RANK)],
        [tall(tile, RANK), whole(1, RANK)],
        [jax.ShapeDtypeStruct((rows, RANK), jnp.float32), jax.ShapeDtypeStruct((1, RANK), jnp.float32)],
        [pltpu.VMEM((RANK, RANK), jnp.bfloat16)] * 2,
        6 * rows * RANK**2,
        8 * rows * RANK,
        "right_and_squares",
        12,
    )(product_full, inverse)


def momentum_kernel(right_ref, ortho_ref, momentum_ref, gradient_ref, out_ref):
    projection = dot16(right_ref[...].astype(jnp.bfloat16), ortho_ref[...], (1, 0))
    out_ref[...] = momentum_ref[...] + gradient_ref[...].astype(jnp.float32) - (1.0 - decay_keep) * projection


def next_momentum(right_full, ortho_high, momentum, gradient):
    rows, columns = momentum.shape
    tile = 256
    return call(
        momentum_kernel,
        (rows // tile,),
        [tall(tile, RANK), whole(RANK, columns), tall(tile, columns), tall(tile, columns)],
        tall(tile, columns),
        jax.ShapeDtypeStruct((rows, columns), jnp.float32),
        [],
        2 * rows * columns * RANK,
        10 * rows * columns,
        "next_momentum",
        20,
    )(right_full, ortho_high, momentum, gradient)


def weight_kernel(right_ref, squares_ref, high_ref, low_ref, weight_ref, basis_ref, out_ref):
    basis = right_ref[...] / jnp.sqrt(squares_ref[...] + norm_eps)
    basis_ref[...] = basis
    update = dot_split(split(basis), (high_ref[...], low_ref[...]), (1, 0))
    scale_step = step_rms * math.sqrt(D * FF / RANK)
    out_ref[...] = (weight_ref[...].astype(jnp.float32) - scale_step * update).astype(jnp.bfloat16)


def next_weight(right_full, squares, ortho, weight):
    rows, columns = weight.shape
    tile = 256
    return call(
        weight_kernel,
        (rows // tile,),
        [tall(tile, RANK), whole(1, RANK), whole(RANK, columns), whole(RANK, columns), tall(tile, columns)],
        [tall(tile, RANK), tall(tile, columns)],
        [jax.ShapeDtypeStruct((rows, RANK), jnp.float32), jax.ShapeDtypeStruct((rows, columns), jnp.bfloat16)],
        [],
        6 * rows * columns * RANK,
        4 * rows * columns + 8 * rows * RANK,
        "next_weight",
        24,
    )(right_full, squares, *ortho, weight)


def exchange(array):
    return lax.all_to_all(array, "col", 0, 0)


def col_scatter(array):
    return jnp.sum(exchange(array.reshape((16, array.shape[0] // 16) + array.shape[1:])), axis=0)


def col_gather(array):
    return exchange(jnp.broadcast_to(array[None], (16,) + array.shape)).reshape((16 * array.shape[0],) + array.shape[1:])


def on_device(momentum, gradient, weight, basis_prev):
    row, col = lax.axis_index("row"), lax.axis_index("col")
    x, core, y, z = row // 2, row % 2, col // 4, col % 4
    given = left_half(jnp.reshape(1 - core, (1,)).astype(jnp.int32), momentum, gradient, basis_prev)
    taken = lax.ppermute(given, "row", other_core)
    kept = left_half(jnp.reshape(core, (1,)).astype(jnp.int32), momentum, gradient, basis_prev)
    size = kept.shape[0] // 4
    sums = [pick(kept, (x + s) % 4, size) + pick(taken, (x + s) % 4, size) for s in range(4)]
    left_rows = total(sums[0], [lax.ppermute(sums[s], "row", along_x(s)) for s in (1, 2, 3)])

    parts = ring_parts(left_rows, along_x)
    gram_rows = core_scatter(dot(left_rows, left_rows, (0, 0), highest), core)
    gram_rows = ring_scatter(ring_scatter(gram_rows, "col", y, along_y), "col", z, along_z)
    parts, gram_rows = lax.optimization_barrier((parts, gram_rows))
    parts = parts + [lax.ppermute(part, "row", other_core) for part in parts]
    place = jnp.stack([x, core]).astype(jnp.int32)
    product, left_full = blended_times_left(place, momentum, gradient, parts)
    left_full = left_full.reshape(-1, RANK)
    got = ring_parts(gram_rows, along_x)
    product, got = lax.optimization_barrier((product, got))
    gram_rows = total(got[0], got[1:])

    count = gram_rows.shape[0]
    gram_copies = jnp.broadcast_to(gram_rows[None], (16,) + gram_rows.shape)
    mixed = exchange(jnp.concatenate([gram_copies, product.reshape(16, -1, RANK)], 1))
    product_full = col_gather(jnp.sum(mixed[:, count:], axis=0))
    inverse = inverse_of_factor(core_gather(mixed[:, :count].reshape(-1, RANK), core))
    ortho = ortho_halves(left_full, inverse)
    ortho, product_full = lax.optimization_barrier((ortho, product_full))

    right_full, squares = right_and_squares(product_full, inverse)
    squares = squares + lax.ppermute(squares, "row", other_core)
    squares = ring_sum(squares, "row", along_x)
    new_momentum = next_momentum(right_full, ortho[0], momentum, gradient)
    new_basis, new_weight = next_weight(right_full, squares, ortho, weight)
    return (new_momentum, new_basis, new_weight)


def solution(mesh):
    return jax.shard_map(
        on_device,
        mesh=mesh,
        in_specs=(P("row", "col"), P("row", "col"), P("row", "col"), P("row", None)),
        out_specs=(P("row", "col"), P("row", None), P("row", "col")),
        check_vma=False,
    )
```
